32 devices in a mesh: gx: 4 (over y, core), gy: 8 (over z, x).
Axes of the slice: x: 2, y: 2, z: 4, core: 2. Of those that a mesh axis runs over, the one named last changes fastest.
Arguments:
- pressure: float32 [128, 256, 128], P('gx', 'gy'), may hold values from -6 to 6
- vel_x: float32 [128, 256, 128], P('gx', 'gy'), may hold values from -6 to 6
- vel_y: float32 [128, 256, 128], P('gx', 'gy'), may hold values from -6 to 6
- vel_z: float32 [128, 256, 128], P('gx', 'gy'), may hold values from -6 to 6
- material: int32 [128, 256, 128], P('gx', 'gy'), may hold values from 0 to 3
- density_table: float32 [4], replicated, may hold values from 0.5 to 4
- speed_table: float32 [4], replicated, may hold values from 0.3 to 1
- panel_vals: float32 [64, 128, 8, 128], P(('gx', 'gy')), may hold values from -6 to 6
- panel_tile: int32 [64, 128, 1], P(('gx', 'gy')), may hold values from 0 to 31; in each aligned block of 256 rows (0 to 255, 256 to 511, ..., all dimensions but the last counted through in order) at most 16 rows name the same one
- panel_cell: int32 [64, 128], P(('gx', 'gy')), may hold values from 0 to 1023
Outputs:
- pressure_out: float32 [128, 256, 128], P('gx', 'gy')
- vel_x_out: float32 [128, 256, 128], P('gx', 'gy')
- vel_y_out: float32 [128, 256, 128], P('gx', 'gy')
- vel_z_out: float32 [128, 256, 128], P('gx', 'gy')
The draws below stay inside these ranges and needn't reach their ends.
Inputs may be any that keep to these rules, and one draw needn't show every extreme that they name: `panel_tile`: among the 256 columns of the panels of one device, no tile is named more than 16 times, a bound that some block reaches.
All inputs are finite; a program needn't handle non-finite values.
Results may differ from the reference program's by a relative error of at most 0.00002.
Values sent between devices are 32-bit elements; how exact they have to be, the bound alone decides.
A program may use at most 64 MiB of HBM per device.

```python
import math
import jax
import jax.numpy as jnp
import numpy as np

CX = 32
CY = 32
NZ = 128
PW = 128
PAN_DEV = 2
STEPS = 8
NMAT = 4
NX = 128
NY = 256
NPAN = 64
CAP = 16
N_GY = 8
DEVICES = 32


def touch_ends(values, key, low, top_value):
    shape = values.shape
    spot = [jax.random.randint(jax.random.fold_in(key, axis), (), 0, shape[axis]) for axis in range(len(shape))]
    values = values.at[tuple(spot)].set(low)
    longest = shape.index(max(shape))
    spot[longest] = (spot[longest] + 1) % shape[longest]
    return values.at[tuple(spot)].set(top_value)


def level_of(key, dims, pieces, smallest, largest):
    def one(position, shards_of):
        heights = jax.random.uniform(jax.random.fold_in(jax.random.fold_in(key, 6), position), (shards_of,), jnp.float32, smallest / len(pieces), largest / len(pieces))
        return jnp.repeat(jnp.exp(heights), dims[position] // shards_of).reshape((-1,) + (1,) * (len(dims) - position - 1))

    gain = one(*pieces[0])
    for cut in pieces[1:]:
        gain = gain * one(*cut)
    return gain


def assign_block(stream_key, own, number, rows, number_of, top, reach, skew):
    sequence = jax.random.permutation(stream_key, number_of)
    packed, usual = load_shares(number_of, rows * top, reach, skew, True), load_shares(number_of, rows * top, reach, skew, False)
    places = jnp.arange(number_of)

    def named(lengths, offset_by):
        used = int((lengths > 0).sum())
        fixed = max(1, used // 4)
        shifted = fixed + (places - fixed + offset_by * (used - fixed)) % max(1, number_of - fixed)
        return jnp.zeros((number_of,), jnp.int32).at[sequence[jnp.where(places < fixed, places, shifted)]].set(jnp.asarray(lengths, jnp.int32))

    lengths = jnp.where(number % 4 == 0, named(packed, number // 4), named(usual, number - number // 4 - 1))
    mixed = jax.random.permutation(jax.random.fold_in(own, 3), number_of)
    source_of, sink = mixed[0:number_of // 2 * 2:2], mixed[1:number_of // 2 * 2:2]
    margin = jnp.minimum(lengths[source_of] - 1, reach - lengths[sink]) // 2
    margin = jnp.where((source_of == sequence[0]) | (sink == sequence[0]) | (lengths[sink] == 0), 0, jnp.maximum(margin, 0))
    shifted = jax.random.randint(jax.random.fold_in(own, 4), (number_of // 2,), 0, 1 << 20) % (margin + 1)
    lengths = lengths.at[source_of].add(-shifted).at[sink].add(shifted)
    labels = jnp.searchsorted(jnp.cumsum(lengths), jnp.arange(rows * top), side="right").astype(jnp.int32)
    listing = labels.reshape(top, rows).T
    listing = listing[jax.random.permutation(jax.random.fold_in(own, 1), rows)]
    offset_by = jax.random.randint(jax.random.fold_in(own, 2), (rows, 1), 0, top)
    return jnp.take_along_axis(listing, (jnp.arange(top)[None, :] + offset_by) % top, axis=1)


def load_shares(count, total, limit, slope, full):
    portions = [(1 << 20) // math.isqrt(grade ** slope) + 1 for grade in range(1, count + 1)]
    largest = limit if full else min(limit, max(-(-total // count), total * portions[0] // sum(portions)))
    least = 1 if total - largest >= count - 1 else 0
    given, rest = [largest] + [least] * (count - 1), total - largest - least * (count - 1)
    while rest > 0:
        free = [i for i in range(1, count) if given[i] < largest] or [i for i in range(1, count) if given[i] < limit]
        mass, left = sum([portions[i] for i in free]), rest
        for i in free:
            extra = min(limit - given[i], max(1, left * portions[i] // mass), rest)
            given[i] = given[i] + extra
            rest = rest - extra
    return np.array(given)


def gaussian(key, dims, scale, bound, cuts=(), kind=jnp.bfloat16):
    drawn = jax.random.normal(key, dims, jnp.float32) * scale
    if len(cuts) > 0:
        drawn = level_of(key, dims, cuts, -0.22, 0.18) * drawn
    return jnp.clip(drawn, min=-bound, max=bound).astype(kind)


def setup_inputs(seed: int = 0) -> dict:
    key_list = jax.random.split(jax.random.key(seed), 11)
    pressure = gaussian(key_list[0], (NX, NY, NZ), 1.0, 6.0, ((0, 4), (1, 8)), jnp.float32)
    vel_x = gaussian(key_list[1], (NX, NY, NZ), 1.0, 6.0, ((0, 4), (1, 8)), jnp.float32)
    vel_y = gaussian(key_list[2], (NX, NY, NZ), 1.0, 6.0, ((0, 4), (1, 8)), jnp.float32)
    vel_z = gaussian(key_list[3], (NX, NY, NZ), 1.0, 6.0, ((0, 4), (1, 8)), jnp.float32)
    material = touch_ends(jax.random.randint(key_list[4], (NX, NY, NZ), 0, NMAT), jax.random.fold_in(key_list[4], 1), 0, NMAT - 1).astype(jnp.int32)
    density_table = jnp.clip(jnp.exp(jax.random.uniform(key_list[5], (NMAT,), jnp.float32, math.log(0.5), math.log(4.0))), 0.5, 4.0)
    speed_table = jnp.clip(jax.random.uniform(key_list[6], (NMAT,), jnp.float32, 0.3, 1.0), 0.3, 1.0)
    panel_vals = gaussian(key_list[7], (NPAN, PW, STEPS, NZ), 1.0, 6.0, ((0, 32),), jnp.float32)
    panel_tile_keys = jax.random.split(jax.random.fold_in(key_list[8], 1), NPAN * PW // (PAN_DEV * PW))
    panel_tile_turns = jax.random.permutation(jax.random.fold_in(key_list[8], 3), NPAN * PW // (PAN_DEV * PW))
    panel_tile = jax.vmap(lambda own, number: assign_block(jax.random.fold_in(key_list[8], 2), own, number, PAN_DEV * PW, DEVICES, 1, CAP, 2))(panel_tile_keys, panel_tile_turns).reshape((NPAN, PW, 1))
    panel_cell = touch_ends(jax.random.randint(key_list[9], (NPAN, PW), 0, CX * CY), jax.random.fold_in(key_list[9], 1), 0, (CX * CY) - 1).astype(jnp.int32)
    return dict(pressure=pressure, vel_x=vel_x, vel_y=vel_y, vel_z=vel_z, material=material, density_table=density_table, speed_table=speed_table, panel_vals=panel_vals, panel_tile=panel_tile, panel_cell=panel_cell)


courant = 0.55


def lookup(material, table):
    total = jnp.zeros(material.shape, jnp.float32)
    for index in range(NMAT):
        total = total + jnp.where(material == index, table[index], 0.0)
    return total


def next_along(field, axis):
    size = field.shape[axis]
    inner = jax.lax.slice_in_dim(field, 1, size, axis=axis)
    zero_plane = jnp.zeros_like(jax.lax.slice_in_dim(field, 0, 1, axis=axis))
    return jnp.concatenate([inner, zero_plane], axis=axis)


def prev_along(field, axis):
    size = field.shape[axis]
    inner = jax.lax.slice_in_dim(field, 0, size - 1, axis=axis)
    zero_plane = jnp.zeros_like(jax.lax.slice_in_dim(field, 0, 1, axis=axis))
    return jnp.concatenate([zero_plane, inner], axis=axis)


def reference(pressure, vel_x, vel_y, vel_z, material, density_table, speed_table, panel_vals, panel_tile, panel_cell):
    density = lookup(material, density_table)
    speed = lookup(material, speed_table)
    buoyancy = 1.0 / density
    stiffness = density * speed * speed
    target = panel_tile.reshape(-1).astype(jnp.int32)
    cell_index = panel_cell.reshape(-1).astype(jnp.int32)
    xs_global = (target // N_GY) * CX + cell_index // CY
    ys_global = (target % N_GY) * CY + cell_index % CY
    values = panel_vals.reshape(-1, STEPS, NZ)
    for step in range(STEPS):
        vel_x = vel_x - courant * buoyancy * (next_along(pressure, 0) - pressure)
        vel_y = vel_y - courant * buoyancy * (next_along(pressure, 1) - pressure)
        vel_z = vel_z - courant * buoyancy * (next_along(pressure, 2) - pressure)
        divergence = (vel_x - prev_along(vel_x, 0)) + (vel_y - prev_along(vel_y, 1))
        divergence = divergence + (vel_z - prev_along(vel_z, 2))
        source = jnp.zeros(pressure.shape, pressure.dtype).at[xs_global, ys_global].add(values[:, step, :])
        pressure = pressure - courant * stiffness * divergence + courant * stiffness * source
    return pressure, vel_x, vel_y, vel_z
```

```python
import functools

import jax
import jax.numpy as jnp
from jax import lax
from jax.experimental import pallas as pl
from jax.experimental.pallas import tpu as pltpu
from jax.sharding import PartitionSpec as P

courant = 0.55
MESH = pl.DeviceIdType.MESH
LANES = 128


def pack_kernel(plan, tile_ref, cell_ref, panel_ref, out_ref, head_ref, count_ref):
    size_x, size_y, slots, per_chunk, rows, group = plan
    devices = size_x * size_y
    columns, steps, layers = panel_ref.shape
    width = cell_ref.shape[1]
    me = lax.axis_index("gx") * size_y + lax.axis_index("gy")
    base = lax.rem(me, group) * rows
    lane = lax.broadcasted_iota(jnp.int32, (1, LANES), 1)

    @pl.loop(0, devices)
    def _(d):
        count_ref[d] = 0
        head_ref[d] = jnp.zeros((1, LANES), jnp.float32)
        for c in range(steps // per_chunk):
            out_ref[c, d] = jnp.zeros((rows, layers), jnp.float32)

    @pl.loop(0, columns)
    def _(c):
        t = tile_ref[c]
        slot = count_ref[t]
        count_ref[t] = slot + 1
        cell = cell_ref[c // width, lax.rem(c, width)]
        number = (cell + 1).astype(jnp.float32)
        spot = lane - (base + slot)
        row = head_ref[t]
        for j in range(per_chunk):
            row = jnp.where(spot == j * slots, number, row)
        head_ref[t] = row
        for s in range(steps):
            out_ref[s // per_chunk, t, pl.ds((s % per_chunk) * slots + slot, 1), :] = panel_ref[c, pl.ds(s, 1), :]


def wave_kernel(
    plan,
    p_in,
    vx_in,
    vy_in,
    vz_in,
    mat_in,
    dens,
    speed,
    send,
    head,
    P_,
    VX,
    VY,
    VZ,
    CB,
    CS,
    recv,
    head_recv,
    onehot,
    rhs,
    source,
    hx_lo,
    hx_hi,
    hy_lo,
    hy_hi,
    x_out,
    y_out,
    vxh,
    cbxh,
    vyh,
    cbyh,
    y_start,
    bulk_send,
    bulk_recv,
    head_sem,
    halo_send,
    halo_recv,
    start_send,
    start_recv,
):
    size_x, size_y, slots, per_chunk, rows, group = plan
    devices = size_x * size_y
    cx, cy, nz = p_in.shape
    chunks = recv.shape[0]
    steps = chunks * per_chunk
    gx, gy = lax.axis_index("gx"), lax.axis_index("gy")
    me = gx * size_y + gy
    has_xl, has_xu = gx > 0, gx < size_x - 1
    has_yl, has_yu = gy > 0, gy < size_y - 1
    x_up, x_down = (gx + 1, gy), (gx - 1, gy)
    y_up, y_down = (gx, gy + 1), (gx, gy - 1)

    barrier = pltpu.get_barrier_semaphore()

    @pl.loop(1, devices)
    def _(k):
        t = lax.rem(me + k, devices)
        pl.semaphore_signal(barrier, inc=1, device_id=(t // size_y, lax.rem(t, size_y)), device_id_type=MESH)

    b_of, k_of = [], []
    for m in range(dens.shape[0]):
        d = jnp.full((1, nz), dens[m], jnp.float32)
        c = jnp.full((1, nz), speed[m], jnp.float32)
        b_of.append(courant * (1.0 / d))
        k_of.append(courant * (d * c * c))

    @pl.loop(0, cx)
    def _(i):
        mat = mat_in[i]
        b = jnp.zeros((cy, nz), jnp.float32)
        k = jnp.zeros((cy, nz), jnp.float32)
        for m in range(dens.shape[0]):
            b = jnp.where(mat == m, b_of[m], b)
            k = jnp.where(mat == m, k_of[m], k)
        CB[i] = b
        CS[i] = k
        p = p_in[i]
        vy = vy_in[i]
        P_[i] = p
        VX[i] = vx_in[i]
        VY[i] = vy
        VZ[i] = vz_in[i]
        y_out[0, 0, pl.ds(i, 1), :] = p[0:1]
        y_out[0, 1, pl.ds(i, 1), :] = p[cy - 1 : cy]
        y_start[0, pl.ds(i, 1), :] = vy[cy - 1 : cy]
        y_start[1, pl.ds(i, 1), :] = b[cy - 1 : cy]

    x_out[0, 0] = p_in[0]
    x_out[0, 1] = p_in[cx - 1]

    @pl.when(jnp.logical_not(has_xl))
    def _():
        vxh[...] = jnp.zeros_like(vxh)
        cbxh[...] = jnp.zeros_like(cbxh)
        hx_lo[...] = jnp.zeros_like(hx_lo)

    @pl.when(jnp.logical_not(has_xu))
    def _():
        hx_hi[...] = jnp.zeros_like(hx_hi)

    @pl.when(jnp.logical_not(has_yl))
    def _():
        vyh[...] = jnp.zeros_like(vyh)
        cbyh[...] = jnp.zeros_like(cbyh)
        hy_lo[...] = jnp.zeros_like(hy_lo)

    @pl.when(jnp.logical_not(has_yu))
    def _():
        hy_hi[...] = jnp.zeros_like(hy_hi)

    pl.semaphore_wait(barrier, devices - 1)

    def remote(src, dst, send_sem, recv_sem, device):
        return pltpu.make_async_remote_copy(
            src_ref=src, dst_ref=dst, send_sem=send_sem, recv_sem=recv_sem, device_id=device, device_id_type=MESH
        )

    def halo(s, direction):
        src, dst, device = (
            (x_out.at[s, 0], hx_hi.at[s], x_down),
            (x_out.at[s, 1], hx_lo.at[s], x_up),
            (y_out.at[s, 0], hy_hi.at[s], y_down),
            (y_out.at[s, 1], hy_lo.at[s], y_up),
        )[direction]
        return remote(src, dst, halo_send.at[s, direction], halo_recv.at[s, direction], device)

    senders = (has_xl, has_xu, has_yl, has_yu)
    receivers = (has_xu, has_xl, has_yu, has_yl)

    def halo_start(s):
        for direction in range(4):

            @pl.when(senders[direction])
            def _():
                halo(s, direction).start()

    def halo_wait(s):
        for direction in range(4):

            @pl.when(receivers[direction])
            def _():
                halo(s, direction).wait_recv()

    def first(which):
        src, dst, device = (
            (vx_in.at[cx - 1], vxh, x_up),
            (CB.at[cx - 1], cbxh, x_up),
            (y_start.at[0], vyh, y_up),
            (y_start.at[1], cbyh, y_up),
        )[which]
        return remote(src, dst, start_send.at[which], start_recv.at[which], device)

    def bulk_start(c):
        pltpu.make_async_copy(send.at[c, me], recv.at[c, me], bulk_recv.at[c]).start()

        @pl.loop(1, devices)
        def _(k):
            t = lax.rem(me + k, devices)
            remote(
                send.at[c, t], recv.at[c, me], bulk_send.at[c], bulk_recv.at[c], (t // size_y, lax.rem(t, size_y))
            ).start()

    halo_start(0)
    for which in range(4):

        @pl.when((has_xu, has_xu, has_yu, has_yu)[which])
        def _():
            first(which).start()

    pltpu.make_async_copy(head.at[me], head_recv.at[me], head_sem.at[1]).start()

    @pl.loop(1, devices)
    def _(k):
        t = lax.rem(me + k, devices)
        remote(
            head.at[t], head_recv.at[me], head_sem.at[0], head_sem.at[1], (t // size_y, lax.rem(t, size_y))
        ).start()

    bulk_start(0)
    if chunks > 1:
        bulk_start(1)

    for which in range(4):

        @pl.when((has_xl, has_xl, has_yl, has_yl)[which])
        def _():
            first(which).wait_recv()

    pltpu.make_async_copy(head_recv, head_recv, head_sem.at[1]).wait()
    block = min(128, cx * cy)
    for r in range(devices // group):
        cells = jnp.sum(head_recv[pl.ds(r * group, group)], axis=0)

        @pl.loop(0, cx * cy // block)
        def _(m):
            number = lax.broadcasted_iota(jnp.int32, (block, LANES), 0) + (m * block + 1)
            onehot[pl.ds(pl.multiple_of(m * block, block), block), r * LANES : (r + 1) * LANES] = jnp.where(
                number.astype(jnp.float32) == cells, 1.0, 0.0
            ).astype(jnp.bfloat16)

    row = lax.broadcasted_iota(jnp.int32, (cy, nz), 0)
    lane = lax.broadcasted_iota(jnp.int32, (cy, nz), 1)

    @pl.loop(0, steps)
    def _(s):
        c = s // per_chunk

        @pl.when(lax.rem(s, per_chunk) == 0)
        def _():
            pltpu.make_async_copy(recv.at[c], recv.at[c], bulk_recv.at[c]).wait()

        @pl.loop(0, devices)
        def _(d):
            values = recv[c, d]
            if per_chunk > 1:
                step_of = lax.broadcasted_iota(jnp.int32, (rows, nz), 0) // slots
                values = jnp.where(step_of == lax.rem(s, per_chunk), values, 0.0)
            high = values.astype(jnp.bfloat16)
            low = (values - high.astype(jnp.float32)).astype(jnp.bfloat16)
            at = pl.ds(pl.multiple_of(d * rows, rows), rows)
            rhs[at, 0:nz] = high
            rhs[at, nz : 2 * nz] = low

        mm = min(256, cx * cy)

        @pl.loop(0, cx * cy // mm)
        def _(m):
            at = pl.ds(pl.multiple_of(m * mm, mm), mm)
            out = jnp.dot(onehot[at, :], rhs[...], preferred_element_type=jnp.float32)
            source[at, :] = out[:, :nz] + out[:, nz:]

        halo_wait(s)

        def plane(i, p, p_next, vx_prev):
            b = CB[i]
            at = pl.ds(i, 1)
            vx = VX[i] - b * (p_next - p)
            p_yn = jnp.where(row == cy - 1, hy_hi[s, at, :], pltpu.roll(p, cy - 1, 0))
            vy = VY[i] - b * (p_yn - p)
            p_zn = jnp.where(lane == nz - 1, 0.0, pltpu.roll(p, nz - 1, 1))
            vz = VZ[i] - b * (p_zn - p)
            edge = vyh[at, :] - cbyh[at, :] * (p[0:1] - hy_lo[s, at, :])
            vyh[at, :] = edge
            vy_prev = jnp.where(row == 0, edge, pltpu.roll(vy, 1, 0))
            vz_prev = jnp.where(lane == 0, 0.0, pltpu.roll(vz, 1, 1))
            divergence = (vx - vx_prev) + (vy - vy_prev)
            divergence = divergence + (vz - vz_prev)
            src = source[pl.ds(pl.multiple_of(i * cy, cy), cy), :]
            new = p + CS[i] * (src - divergence)
            VX[i] = vx
            VY[i] = vy
            VZ[i] = vz
            P_[i] = new

            @pl.when(s < steps - 1)
            def _():
                y_out[s + 1, 0, at, :] = new[0:1]
                y_out[s + 1, 1, at, :] = new[cy - 1 : cy]

            return new, vx

        p0 = P_[0]
        edge_x = vxh[...] - cbxh[...] * (p0 - hx_lo[s])
        vxh[...] = edge_x

        def body(i, carry):
            p, vx_prev = carry
            p_next = P_[i + 1]
            _, vx = plane(i, p, p_next, vx_prev)
            return p_next, vx

        p_last, vx_last = lax.fori_loop(0, cx - 1, body, (p0, edge_x))
        new_last, _ = plane(cx - 1, p_last, hx_hi[s], vx_last)

        @pl.when(s < steps - 1)
        def _():
            x_out[s + 1, 0] = P_[0]
            x_out[s + 1, 1] = new_last
            halo_start(s + 1)

        @pl.when(jnp.logical_and(lax.rem(s, per_chunk) == per_chunk - 1, c + 2 < chunks))
        def _():
            bulk_start(c + 2)

    others = devices - 1
    pltpu.make_async_copy(head.at[pl.ds(0, others)], head.at[pl.ds(0, others)], head_sem.at[0]).wait()

    @pl.loop(0, chunks)
    def _(c):
        whole = send.at[c, pl.ds(0, others)]
        pltpu.make_async_copy(whole, whole, bulk_send.at[c]).wait()

    @pl.loop(0, steps)
    def _(s):
        for direction in range(4):

            @pl.when(senders[direction])
            def _():
                halo(s, direction).wait_send()

    for which in range(4):

        @pl.when((has_xu, has_xu, has_yu, has_yu)[which])
        def _():
            first(which).wait_send()


def per_device(pressure, vel_x, vel_y, vel_z, material, density_table, speed_table, panel_vals, panel_tile, panel_cell):
    size_x = lax.axis_size("gx")
    size_y = lax.axis_size("gy")
    devices = size_x * size_y
    cx, cy, nz = pressure.shape
    steps = panel_vals.shape[2]
    columns = panel_vals.shape[0] * panel_vals.shape[1]
    slots = max(2, 2 * columns // devices)
    per_chunk = max(1, 8 // slots)
    rows = slots * per_chunk
    chunks = steps // per_chunk
    group = LANES // rows
    plan = (size_x, size_y, slots, per_chunk, rows, group)
    f32 = jnp.float32
    vmem = pl.BlockSpec(memory_space=pltpu.VMEM)
    smem = pl.BlockSpec(memory_space=pltpu.SMEM)
    send, head = pl.pallas_call(
        functools.partial(pack_kernel, plan),
        out_shape=(
            jax.ShapeDtypeStruct((chunks, devices, rows, nz), f32),
            jax.ShapeDtypeStruct((devices, 1, LANES), f32),
        ),
        in_specs=[smem, smem, vmem],
        out_specs=(vmem, vmem),
        scratch_shapes=[pltpu.SMEM((devices,), jnp.int32)],
        compiler_params=pltpu.CompilerParams(vmem_limit_bytes=16 * 1024 * 1024),
        name="pack",
    )(panel_tile.reshape(-1), panel_cell, panel_vals.reshape(columns, steps, nz))
    field = jax.ShapeDtypeStruct((cx, cy, nz), f32)
    dma = pltpu.SemaphoreType.DMA
    return pl.pallas_call(
        functools.partial(wave_kernel, plan),
        out_shape=(field,) * 4,
        in_specs=[vmem] * 5 + [smem] * 2 + [vmem] * 2,
        out_specs=(vmem,) * 4,
        scratch_shapes=[
            pltpu.VMEM((cx, cy, nz), f32),
            pltpu.VMEM((cx, cy, nz), f32),
            pltpu.VMEM((chunks, devices, rows, nz), f32),
            pltpu.VMEM((devices, 1, LANES), f32),
            pltpu.VMEM((cx * cy, devices * rows), jnp.bfloat16),
            pltpu.VMEM((devices * rows, 2 * nz), jnp.bfloat16),
            pltpu.VMEM((cx * cy, nz), f32),
            pltpu.VMEM((steps, cy, nz), f32),
            pltpu.VMEM((steps, cy, nz), f32),
            pltpu.VMEM((steps, cx, nz), f32),
            pltpu.VMEM((steps, cx, nz), f32),
            pltpu.VMEM((steps, 2, cy, nz), f32),
            pltpu.VMEM((steps, 2, cx, nz), f32),
            pltpu.VMEM((cy, nz), f32),
            pltpu.VMEM((cy, nz), f32),
            pltpu.VMEM((cx, nz), f32),
            pltpu.VMEM((cx, nz), f32),
            pltpu.VMEM((2, cx, nz), f32),
            dma((chunks,)),
            dma((chunks,)),
            dma((2,)),
            dma((steps, 4)),
            dma((steps, 4)),
            dma((4,)),
            dma((4,)),
        ],
        compiler_params=pltpu.CompilerParams(
            collective_id=0, has_side_effects=True, vmem_limit_bytes=40 * 1024 * 1024
        ),
        name="wave",
    )(pressure, vel_x, vel_y, vel_z, material, density_table, speed_table, send, head)


def solution(mesh):
    tile = P("gx", "gy", None)
    return jax.shard_map(
        per_device,
        mesh=mesh,
        in_specs=(
            tile,
            tile,
            tile,
            tile,
            tile,
            P(),
            P(),
            P(("gx", "gy"), None, None, None),
            P(("gx", "gy"), None, None),
            P(("gx", "gy"), None),
        ),
        out_specs=(tile,) * 4,
        check_vma=False,
    )
```

```python
import functools

import jax
import jax.numpy as jnp
from jax import lax
from jax.experimental import pallas as pl
from jax.experimental.pallas import tpu as pltpu
from jax.sharding import PartitionSpec as P

courant = 0.55
MESH = pl.DeviceIdType.MESH
LANES = 128


def pack_kernel(plan, tile_ref, cell_ref, panel_ref, out_ref, head_ref, count_ref):
    size_x, size_y, slots, per_chunk, rows, group = plan
    devices = size_x * size_y
    columns, steps, layers = panel_ref.shape
    width = cell_ref.shape[1]
    me = lax.axis_index("gx") * size_y + lax.axis_index("gy")
    base = lax.rem(me, group) * rows
    lane = lax.broadcasted_iota(jnp.int32, (1, LANES), 1)

    @pl.loop(0, devices)
    def _(d):
        count_ref[d] = 0
        head_ref[d] = jnp.zeros((1, LANES), jnp.float32)
        for c in range(steps // per_chunk):
            out_ref[c, d] = jnp.zeros((rows, layers), jnp.float32)

    @pl.loop(0, columns)
    def _(c):
        t = tile_ref[c]
        slot = count_ref[t]
        count_ref[t] = slot + 1
        cell = cell_ref[c // width, lax.rem(c, width)]
        number = (cell + 1).astype(jnp.float32)
        spot = lane - (base + slot)
        row = head_ref[t]
        for j in range(per_chunk):
            row = jnp.where(spot == j * slots, number, row)
        head_ref[t] = row
        for s in range(steps):
            out_ref[s // per_chunk, t, pl.ds((s % per_chunk) * slots + slot, 1), :] = panel_ref[c, pl.ds(s, 1), :]


def wave_kernel(
    plan,
    p_in,
    vx_in,
    vy_in,
    vz_in,
    mat_in,
    dens,
    speed,
    send,
    head,
    P_,
    VX,
    VY,
    VZ,
    mat,
    CB,
    CS,
    recv,
    head_recv,
    onehot,
    rhs,
    source,
    hx_lo,
    hx_hi,
    hy_lo,
    hy_hi,
    x_out,
    y_out,
    vxh,
    cbxh,
    vyh,
    cbyh,
    x_start,
    y_start,
    load_sem,
    bulk_send,
    bulk_recv,
    head_sem,
    halo_send,
    halo_recv,
    start_send,
    start_recv,
):
    size_x, size_y, slots, per_chunk, rows, group = plan
    devices = size_x * size_y
    cx, cy, nz = p_in.shape
    chunks = recv.shape[0]
    steps = chunks * per_chunk
    planes = 8 if cx % 8 == 0 else 1
    gx, gy = lax.axis_index("gx"), lax.axis_index("gy")
    me = gx * size_y + gy
    has_xl, has_xu = gx > 0, gx < size_x - 1
    has_yl, has_yu = gy > 0, gy < size_y - 1
    x_up, x_down = (gx + 1, gy), (gx - 1, gy)
    y_up, y_down = (gx, gy + 1), (gx, gy - 1)

    loads = [
        pltpu.make_async_copy(src, dst, load_sem.at[n])
        for n, (src, dst) in enumerate(((mat_in, mat), (p_in, P_), (vy_in, VY), (vx_in, VX), (vz_in, VZ)))
    ]
    for load in loads:
        load.start()

    barrier = pltpu.get_barrier_semaphore()

    @pl.loop(1, devices)
    def _(k):
        t = lax.rem(me + k, devices)
        pl.semaphore_signal(barrier, inc=1, device_id=(t // size_y, lax.rem(t, size_y)), device_id_type=MESH)

    @pl.when(jnp.logical_not(has_xl))
    def _():
        vxh[...] = jnp.zeros_like(vxh)
        cbxh[...] = jnp.zeros_like(cbxh)
        hx_lo[...] = jnp.zeros_like(hx_lo)

    @pl.when(jnp.logical_not(has_xu))
    def _():
        hx_hi[...] = jnp.zeros_like(hx_hi)

    @pl.when(jnp.logical_not(has_yl))
    def _():
        vyh[...] = jnp.zeros_like(vyh)
        cbyh[...] = jnp.zeros_like(cbyh)
        hy_lo[...] = jnp.zeros_like(hy_lo)

    @pl.when(jnp.logical_not(has_yu))
    def _():
        hy_hi[...] = jnp.zeros_like(hy_hi)

    pl.semaphore_wait(barrier, devices - 1)

    def remote(src, dst, send_sem, recv_sem, device):
        return pltpu.make_async_remote_copy(
            src_ref=src, dst_ref=dst, send_sem=send_sem, recv_sem=recv_sem, device_id=device, device_id_type=MESH
        )

    def halo(s, direction):
        src, dst, device = (
            (x_out.at[s, 0], hx_hi.at[s], x_down),
            (x_out.at[s, 1], hx_lo.at[s], x_up),
            (y_out.at[s, 0], hy_hi.at[s], y_down),
            (y_out.at[s, 1], hy_lo.at[s], y_up),
        )[direction]
        return remote(src, dst, halo_send.at[s, direction], halo_recv.at[s, direction], device)

    senders = (has_xl, has_xu, has_yl, has_yu)
    receivers = (has_xu, has_xl, has_yu, has_yl)

    def halo_start(s):
        for direction in range(4):

            @pl.when(senders[direction])
            def _():
                halo(s, direction).start()

    def halo_wait(s):
        for direction in range(4):

            @pl.when(receivers[direction])
            def _():
                halo(s, direction).wait_recv()

    def first(which):
        src, dst, device = (
            (x_start, vxh, x_up),
            (CB.at[cx - 1], cbxh, x_up),
            (y_start.at[0], vyh, y_up),
            (y_start.at[1], cbyh, y_up),
        )[which]
        return remote(src, dst, start_send.at[which], start_recv.at[which], device)

    def bulk_start(c):
        pltpu.make_async_copy(send.at[c, me], recv.at[c, me], bulk_recv.at[c]).start()

        @pl.loop(1, devices)
        def _(k):
            t = lax.rem(me + k, devices)
            remote(
                send.at[c, t], recv.at[c, me], bulk_send.at[c], bulk_recv.at[c], (t // size_y, lax.rem(t, size_y))
            ).start()

    pltpu.make_async_copy(head.at[me], head_recv.at[me], head_sem.at[1]).start()

    @pl.loop(1, devices)
    def _(k):
        t = lax.rem(me + k, devices)
        remote(
            head.at[t], head_recv.at[me], head_sem.at[0], head_sem.at[1], (t // size_y, lax.rem(t, size_y))
        ).start()

    bulk_start(0)
    b_of, k_of = [], []
    for m in range(dens.shape[0]):
        d = jnp.full((1, nz), dens[m], jnp.float32)
        c = jnp.full((1, nz), speed[m], jnp.float32)
        b_of.append(courant * (1.0 / d))
        k_of.append(courant * (d * c * c))

    for load in loads[:3]:
        load.wait()

    @pl.loop(0, cx // planes)
    def _(g):
        at = pl.ds(g * planes, planes)
        material = mat[at]
        b = jnp.zeros(material.shape, jnp.float32)
        k = jnp.zeros(material.shape, jnp.float32)
        for m in range(dens.shape[0]):
            b = jnp.where(material == m, b_of[m][None], b)
            k = jnp.where(material == m, k_of[m][None], k)
        CB[at] = b
        CS[at] = k
        p = P_[at]
        y_out[0, 0, at] = p[:, 0:1]
        y_out[0, 1, at] = p[:, cy - 1 : cy]
        y_start[0, at] = VY[at][:, cy - 1 : cy]
        y_start[1, at] = b[:, cy - 1 : cy]

    x_out[0, 0] = P_[0]
    x_out[0, 1] = P_[cx - 1]
    for load in loads[3:]:
        load.wait()
    x_start[...] = VX[cx - 1]

    halo_start(0)
    for which in range(4):

        @pl.when((has_xu, has_xu, has_yu, has_yu)[which])
        def _():
            first(which).start()

    if chunks > 1:
        bulk_start(1)

    for which in range(4):

        @pl.when((has_xl, has_xl, has_yl, has_yl)[which])
        def _():
            first(which).wait_recv()

    pltpu.make_async_copy(head_recv, head_recv, head_sem.at[1]).wait()
    block = min(128, cx * cy)
    for r in range(devices // group):
        cells = jnp.sum(head_recv[pl.ds(r * group, group)], axis=0)

        @pl.loop(0, cx * cy // block)
        def _(m):
            number = lax.broadcasted_iota(jnp.int32, (block, LANES), 0) + (m * block + 1)
            onehot[pl.ds(pl.multiple_of(m * block, block), block), r * LANES : (r + 1) * LANES] = jnp.where(
                number.astype(jnp.float32) == cells, 1.0, 0.0
            ).astype(jnp.bfloat16)

    row = lax.broadcasted_iota(jnp.int32, (planes, cy, nz), 1)
    lane = lax.broadcasted_iota(jnp.int32, (planes, cy, nz), 2)

    @pl.loop(0, steps)
    def _(s):
        c = s // per_chunk

        @pl.when(lax.rem(s, per_chunk) == 0)
        def _():
            pltpu.make_async_copy(recv.at[c], recv.at[c], bulk_recv.at[c]).wait()

        values = recv[c].reshape(devices * rows, nz)
        if per_chunk > 1:
            step_of = lax.rem(lax.broadcasted_iota(jnp.int32, values.shape, 0), rows) // slots
            values = jnp.where(step_of == lax.rem(s, per_chunk), values, 0.0)
        high = values.astype(jnp.bfloat16)
        rhs[:, 0:nz] = high
        rhs[:, nz : 2 * nz] = (values - high.astype(jnp.float32)).astype(jnp.bfloat16)

        mm = min(256, cx * cy)

        @pl.loop(0, cx * cy // mm)
        def _(m):
            at = pl.ds(pl.multiple_of(m * mm, mm), mm)
            out = jnp.dot(onehot[at, :], rhs[...], preferred_element_type=jnp.float32)
            source[at, :] = out[:, :nz] + out[:, nz:]

        halo_wait(s)

        def block_of(i, after, vx_before):
            at = pl.ds(i, planes)
            b = CB[at]
            p = P_[at]
            p_xn = jnp.concatenate([p[1:], after[None]], axis=0)
            vx = VX[at] - b * (p_xn - p)
            p_yn = jnp.where(row == cy - 1, hy_hi[s, at], pltpu.roll(p, cy - 1, 1))
            vy = VY[at] - b * (p_yn - p)
            p_zn = jnp.where(lane == nz - 1, 0.0, pltpu.roll(p, nz - 1, 2))
            vz = VZ[at] - b * (p_zn - p)
            edge = vyh[at] - cbyh[at] * (p[:, 0:1] - hy_lo[s, at])
            vx_prev = jnp.concatenate([vx_before[None], vx[:-1]], axis=0)
            vy_prev = jnp.where(row == 0, edge, pltpu.roll(vy, 1, 1))
            vz_prev = jnp.where(lane == 0, 0.0, pltpu.roll(vz, 1, 2))
            divergence = (vx - vx_prev) + (vy - vy_prev)
            divergence = divergence + (vz - vz_prev)
            src = source[pl.ds(pl.multiple_of(i * cy, cy), planes * cy), :].reshape(planes, cy, nz)
            new = p + CS[at] * (src - divergence)
            vyh[at] = edge
            VX[at] = vx
            VY[at] = vy
            VZ[at] = vz
            P_[at] = new
            y_out[s + 1, 0, at] = new[:, 0:1]
            y_out[s + 1, 1, at] = new[:, cy - 1 : cy]
            return vx[planes - 1]

        edge_x = vxh[...] - cbxh[...] * (P_[0] - hx_lo[s])
        vxh[...] = edge_x

        def body(g, vx_before):
            return block_of(g * planes, P_[(g + 1) * planes], vx_before)

        vx_last = lax.fori_loop(0, cx // planes - 1, body, edge_x)
        block_of(cx - planes, hx_hi[s], vx_last)

        @pl.when(s < steps - 1)
        def _():
            x_out[s + 1, 0] = P_[0]
            x_out[s + 1, 1] = P_[cx - 1]
            halo_start(s + 1)

        @pl.when(jnp.logical_and(lax.rem(s, per_chunk) == per_chunk - 1, c + 2 < chunks))
        def _():
            bulk_start(c + 2)

    others = devices - 1
    pltpu.make_async_copy(head.at[pl.ds(0, others)], head.at[pl.ds(0, others)], head_sem.at[0]).wait()

    @pl.loop(0, chunks)
    def _(c):
        whole = send.at[c, pl.ds(0, others)]
        pltpu.make_async_copy(whole, whole, bulk_send.at[c]).wait()

    @pl.loop(0, steps)
    def _(s):
        for direction in range(4):

            @pl.when(senders[direction])
            def _():
                halo(s, direction).wait_send()

    for which in range(4):

        @pl.when((has_xu, has_xu, has_yu, has_yu)[which])
        def _():
            first(which).wait_send()


def per_device(pressure, vel_x, vel_y, vel_z, material, density_table, speed_table, panel_vals, panel_tile, panel_cell):
    size_x = lax.axis_size("gx")
    size_y = lax.axis_size("gy")
    devices = size_x * size_y
    cx, cy, nz = pressure.shape
    steps = panel_vals.shape[2]
    columns = panel_vals.shape[0] * panel_vals.shape[1]
    slots = max(2, 2 * columns // devices)
    per_chunk = max(1, 8 // slots)
    rows = slots * per_chunk
    chunks = steps // per_chunk
    group = LANES // rows
    plan = (size_x, size_y, slots, per_chunk, rows, group)
    f32 = jnp.float32
    vmem = pl.BlockSpec(memory_space=pltpu.VMEM)
    smem = pl.BlockSpec(memory_space=pltpu.SMEM)
    hbm = pl.BlockSpec(memory_space=pltpu.HBM)
    send, head = pl.pallas_call(
        functools.partial(pack_kernel, plan),
        out_shape=(
            jax.ShapeDtypeStruct((chunks, devices, rows, nz), f32),
            jax.ShapeDtypeStruct((devices, 1, LANES), f32),
        ),
        in_specs=[smem, smem, vmem],
        out_specs=(vmem, vmem),
        scratch_shapes=[pltpu.SMEM((devices,), jnp.int32)],
        compiler_params=pltpu.CompilerParams(vmem_limit_bytes=16 * 1024 * 1024),
        name="pack",
    )(panel_tile.reshape(-1), panel_cell, panel_vals.reshape(columns, steps, nz))
    field = jax.ShapeDtypeStruct((cx, cy, nz), f32)
    dma = pltpu.SemaphoreType.DMA
    return pl.pallas_call(
        functools.partial(wave_kernel, plan),
        out_shape=(field,) * 4,
        in_specs=[hbm] * 5 + [smem] * 2 + [vmem] * 2,
        out_specs=(vmem,) * 4,
        scratch_shapes=[
            pltpu.VMEM((cx, cy, nz), jnp.int32),
            pltpu.VMEM((cx, cy, nz), f32),
            pltpu.VMEM((cx, cy, nz), f32),
            pltpu.VMEM((chunks, devices, rows, nz), f32),
            pltpu.VMEM((devices, 1, LANES), f32),
            pltpu.VMEM((cx * cy, devices * rows), jnp.bfloat16),
            pltpu.VMEM((devices * rows, 2 * nz), jnp.bfloat16),
            pltpu.VMEM((cx * cy, nz), f32),
            pltpu.VMEM((steps, cy, nz), f32),
            pltpu.VMEM((steps, cy, nz), f32),
            pltpu.VMEM((steps, cx, 1, nz), f32),
            pltpu.VMEM((steps, cx, 1, nz), f32),
            pltpu.VMEM((steps, 2, cy, nz), f32),
            pltpu.VMEM((steps + 1, 2, cx, 1, nz), f32),
            pltpu.VMEM((cy, nz), f32),
            pltpu.VMEM((cy, nz), f32),
            pltpu.VMEM((cx, 1, nz), f32),
            pltpu.VMEM((cx, 1, nz), f32),
            pltpu.VMEM((cy, nz), f32),
            pltpu.VMEM((2, cx, 1, nz), f32),
            dma((5,)),
            dma((chunks,)),
            dma((chunks,)),
            dma((2,)),
            dma((steps, 4)),
            dma((steps, 4)),
            dma((4,)),
            dma((4,)),
        ],
        compiler_params=pltpu.CompilerParams(
            collective_id=0, has_side_effects=True, vmem_limit_bytes=40 * 1024 * 1024
        ),
        name="wave",
    )(pressure, vel_x, vel_y, vel_z, material, density_table, speed_table, send, head)


def solution(mesh):
    tile = P("gx", "gy", None)
    return jax.shard_map(
        per_device,
        mesh=mesh,
        in_specs=(
            tile,
            tile,
            tile,
            tile,
            tile,
            P(),
            P(),
            P(("gx", "gy"), None, None, None),
            P(("gx", "gy"), None, None),
            P(("gx", "gy"), None),
        ),
        out_specs=(tile,) * 4,
        check_vma=False,
    )
```

```python
import functools

import jax
import jax.numpy as jnp
from jax import lax
from jax.experimental import pallas as pl
from jax.experimental.pallas import tpu as pltpu
from jax.sharding import PartitionSpec as P

courant = 0.55
MESH = pl.DeviceIdType.MESH
LANES = 128


def pack_kernel(plan, tile_ref, cell_ref, panel_ref, out_ref, head_ref, count_ref):
    size_x, size_y, slots, per_chunk, rows, group = plan
    devices = size_x * size_y
    columns, steps, layers = panel_ref.shape
    width = cell_ref.shape[1]
    me = lax.axis_index("gx") * size_y + lax.axis_index("gy")
    base = lax.rem(me, group) * rows
    lane = lax.broadcasted_iota(jnp.int32, (1, LANES), 1)

    @pl.loop(0, devices, unroll=4)
    def _(d):
        count_ref[d] = 0
        head_ref[d] = jnp.zeros((1, LANES), jnp.float32)
        for c in range(steps // per_chunk):
            out_ref[c, d] = jnp.zeros((rows, layers), jnp.float32)

    @pl.loop(0, columns, unroll=8)
    def _(c):
        t = tile_ref[c]
        slot = count_ref[t]
        count_ref[t] = slot + 1
        cell = cell_ref[c // width, lax.rem(c, width)]
        number = (cell + 1).astype(jnp.float32)
        spot = lane - (base + slot)
        row = head_ref[t]
        for j in range(per_chunk):
            row = jnp.where(spot == j * slots, number, row)
        head_ref[t] = row
        for s in range(steps):
            out_ref[s // per_chunk, t, pl.ds((s % per_chunk) * slots + slot, 1), :] = panel_ref[c, pl.ds(s, 1), :]


def wave_kernel(
    plan,
    p_in,
    vx_in,
    vy_in,
    vz_in,
    mat_in,
    dens,
    speed,
    send,
    head,
    P_,
    VX,
    VY,
    VZ,
    mat,
    CB,
    CS,
    recv,
    head_recv,
    onehot,
    rhs,
    source,
    hx_lo,
    hx_hi,
    hy_lo,
    hy_hi,
    x_out,
    y_out,
    vxh,
    cbxh,
    vyh,
    cbyh,
    x_start,
    y_start,
    load_sem,
    bulk_send,
    bulk_recv,
    head_sem,
    halo_send,
    halo_recv,
    start_send,
    start_recv,
):
    size_x, size_y, slots, per_chunk, rows, group = plan
    devices = size_x * size_y
    cx, cy, nz = p_in.shape
    chunks = recv.shape[0]
    steps = chunks * per_chunk
    planes = 8 if cx % 8 == 0 else 1
    gx, gy = lax.axis_index("gx"), lax.axis_index("gy")
    me = gx * size_y + gy
    has_xl, has_xu = gx > 0, gx < size_x - 1
    has_yl, has_yu = gy > 0, gy < size_y - 1
    x_up, x_down = (gx + 1, gy), (gx - 1, gy)
    y_up, y_down = (gx, gy + 1), (gx, gy - 1)

    loads = [
        pltpu.make_async_copy(src, dst, load_sem.at[n])
        for n, (src, dst) in enumerate(((mat_in, mat), (p_in, P_), (vy_in, VY), (vx_in, VX), (vz_in, VZ)))
    ]
    for load in loads:
        load.start()

    barrier = pltpu.get_barrier_semaphore()

    @pl.loop(1, devices)
    def _(k):
        t = lax.rem(me + k, devices)
        pl.semaphore_signal(barrier, inc=1, device_id=(t // size_y, lax.rem(t, size_y)), device_id_type=MESH)

    @pl.when(jnp.logical_not(has_xl))
    def _():
        vxh[...] = jnp.zeros_like(vxh)
        cbxh[...] = jnp.zeros_like(cbxh)
        hx_lo[...] = jnp.zeros_like(hx_lo)

    @pl.when(jnp.logical_not(has_xu))
    def _():
        hx_hi[...] = jnp.zeros_like(hx_hi)

    @pl.when(jnp.logical_not(has_yl))
    def _():
        vyh[...] = jnp.zeros_like(vyh)
        cbyh[...] = jnp.zeros_like(cbyh)
        hy_lo[...] = jnp.zeros_like(hy_lo)

    @pl.when(jnp.logical_not(has_yu))
    def _():
        hy_hi[...] = jnp.zeros_like(hy_hi)

    pl.semaphore_wait(barrier, devices - 1)

    def remote(src, dst, send_sem, recv_sem, device):
        return pltpu.make_async_remote_copy(
            src_ref=src, dst_ref=dst, send_sem=send_sem, recv_sem=recv_sem, device_id=device, device_id_type=MESH
        )

    def halo(s, direction):
        src, dst, device = (
            (x_out.at[s, 0], hx_hi.at[s], x_down),
            (x_out.at[s, 1], hx_lo.at[s], x_up),
            (y_out.at[s, 0], hy_hi.at[s], y_down),
            (y_out.at[s, 1], hy_lo.at[s], y_up),
        )[direction]
        return remote(src, dst, halo_send.at[s, direction], halo_recv.at[s, direction], device)

    senders = (has_xl, has_xu, has_yl, has_yu)
    receivers = (has_xu, has_xl, has_yu, has_yl)

    def halo_start(s):
        for direction in range(4):

            @pl.when(senders[direction])
            def _():
                halo(s, direction).start()

    def halo_wait(s):
        for direction in range(4):

            @pl.when(receivers[direction])
            def _():
                halo(s, direction).wait_recv()

    def first(which):
        src, dst, device = (
            (x_start, vxh, x_up),
            (CB.at[cx - 1], cbxh, x_up),
            (y_start.at[0], vyh, y_up),
            (y_start.at[1], cbyh, y_up),
        )[which]
        return remote(src, dst, start_send.at[which], start_recv.at[which], device)

    def bulk_start(c):
        pltpu.make_async_copy(send.at[c, me], recv.at[c, me], bulk_recv.at[c]).start()

        @pl.loop(1, devices)
        def _(k):
            t = lax.rem(me + k, devices)
            remote(
                send.at[c, t], recv.at[c, me], bulk_send.at[c], bulk_recv.at[c], (t // size_y, lax.rem(t, size_y))
            ).start()

    pltpu.make_async_copy(head.at[me], head_recv.at[me], head_sem.at[1]).start()

    @pl.loop(1, devices)
    def _(k):
        t = lax.rem(me + k, devices)
        remote(
            head.at[t], head_recv.at[me], head_sem.at[0], head_sem.at[1], (t // size_y, lax.rem(t, size_y))
        ).start()

    bulk_start(0)
    b_of, k_of = [], []
    for m in range(dens.shape[0]):
        d = jnp.full((1, nz), dens[m], jnp.float32)
        c = jnp.full((1, nz), speed[m], jnp.float32)
        b_of.append(courant * (1.0 / d))
        k_of.append(courant * (d * c * c))

    for load in loads[:3]:
        load.wait()

    @pl.loop(0, cx // planes)
    def _(g):
        at = pl.ds(g * planes, planes)
        material = mat[at]
        b = jnp.zeros(material.shape, jnp.float32)
        k = jnp.zeros(material.shape, jnp.float32)
        for m in range(dens.shape[0]):
            b = jnp.where(material == m, b_of[m][None], b)
            k = jnp.where(material == m, k_of[m][None], k)
        CB[at] = b
        CS[at] = k
        p = P_[at]
        y_out[0, 0, at] = p[:, 0:1]
        y_out[0, 1, at] = p[:, cy - 1 : cy]
        y_start[0, at] = VY[at][:, cy - 1 : cy]
        y_start[1, at] = b[:, cy - 1 : cy]

    x_out[0, 0] = P_[0]
    x_out[0, 1] = P_[cx - 1]
    for load in loads[3:]:
        load.wait()
    x_start[...] = VX[cx - 1]

    halo_start(0)
    for which in range(4):

        @pl.when((has_xu, has_xu, has_yu, has_yu)[which])
        def _():
            first(which).start()

    if chunks > 1:
        bulk_start(1)

    for which in range(4):

        @pl.when((has_xl, has_xl, has_yl, has_yl)[which])
        def _():
            first(which).wait_recv()

    pltpu.make_async_copy(head_recv, head_recv, head_sem.at[1]).wait()
    block = min(128, cx * cy)
    for r in range(devices // group):
        cells = jnp.sum(head_recv[pl.ds(r * group, group)], axis=0)

        @pl.loop(0, cx * cy // block)
        def _(m):
            number = lax.broadcasted_iota(jnp.int32, (block, LANES), 0) + (m * block + 1)
            onehot[pl.ds(pl.multiple_of(m * block, block), block), r * LANES : (r + 1) * LANES] = jnp.where(
                number.astype(jnp.float32) == cells, 1.0, 0.0
            ).astype(jnp.bfloat16)

    row = lax.broadcasted_iota(jnp.int32, (planes, cy, nz), 1)
    lane = lax.broadcasted_iota(jnp.int32, (planes, cy, nz), 2)

    @pl.loop(0, steps)
    def _(s):
        c = s // per_chunk

        @pl.when(lax.rem(s, per_chunk) == 0)
        def _():
            pltpu.make_async_copy(recv.at[c], recv.at[c], bulk_recv.at[c]).wait()

        values = recv[c].reshape(devices * rows, nz)
        if per_chunk > 1:
            step_of = lax.rem(lax.broadcasted_iota(jnp.int32, values.shape, 0), rows) // slots
            values = jnp.where(step_of == lax.rem(s, per_chunk), values, 0.0)
        high = values.astype(jnp.bfloat16)
        rhs[:, 0:nz] = high
        rhs[:, nz : 2 * nz] = (values - high.astype(jnp.float32)).astype(jnp.bfloat16)

        mm = min(256, cx * cy)

        @pl.loop(0, cx * cy // mm)
        def _(m):
            at = pl.ds(pl.multiple_of(m * mm, mm), mm)
            out = jnp.dot(onehot[at, :], rhs[...], preferred_element_type=jnp.float32)
            source[at, :] = out[:, :nz] + out[:, nz:]

        halo_wait(s)

        def block_of(i, after, vx_before):
            at = pl.ds(i, planes)
            b = CB[at]
            p = P_[at]
            p_xn = jnp.concatenate([p[1:], after[None]], axis=0)
            vx = VX[at] - b * (p_xn - p)
            p_yn = jnp.where(row == cy - 1, hy_hi[s, at], pltpu.roll(p, cy - 1, 1))
            vy = VY[at] - b * (p_yn - p)
            p_zn = jnp.where(lane == nz - 1, 0.0, pltpu.roll(p, nz - 1, 2))
            vz = VZ[at] - b * (p_zn - p)
            edge = vyh[at] - cbyh[at] * (p[:, 0:1] - hy_lo[s, at])
            vx_prev = jnp.concatenate([vx_before[None], vx[:-1]], axis=0)
            vy_prev = jnp.where(row == 0, edge, pltpu.roll(vy, 1, 1))
            vz_prev = jnp.where(lane == 0, 0.0, pltpu.roll(vz, 1, 2))
            divergence = (vx - vx_prev) + (vy - vy_prev)
            divergence = divergence + (vz - vz_prev)
            src = source[pl.ds(pl.multiple_of(i * cy, cy), planes * cy), :].reshape(planes, cy, nz)
            new = p + CS[at] * (src - divergence)
            vyh[at] = edge
            VX[at] = vx
            VY[at] = vy
            VZ[at] = vz
            P_[at] = new
            y_out[s + 1, 0, at] = new[:, 0:1]
            y_out[s + 1, 1, at] = new[:, cy - 1 : cy]
            return vx[planes - 1]

        edge_x = vxh[...] - cbxh[...] * (P_[0] - hx_lo[s])
        vxh[...] = edge_x

        def body(g, vx_before):
            return block_of(g * planes, P_[(g + 1) * planes], vx_before)

        vx_last = lax.fori_loop(0, cx // planes - 1, body, edge_x)
        block_of(cx - planes, hx_hi[s], vx_last)

        @pl.when(s < steps - 1)
        def _():
            x_out[s + 1, 0] = P_[0]
            x_out[s + 1, 1] = P_[cx - 1]
            halo_start(s + 1)

        @pl.when(jnp.logical_and(lax.rem(s, per_chunk) == per_chunk - 1, c + 2 < chunks))
        def _():
            bulk_start(c + 2)

    others = devices - 1
    pltpu.make_async_copy(head.at[pl.ds(0, others)], head.at[pl.ds(0, others)], head_sem.at[0]).wait()

    @pl.loop(0, chunks)
    def _(c):
        whole = send.at[c, pl.ds(0, others)]
        pltpu.make_async_copy(whole, whole, bulk_send.at[c]).wait()

    @pl.loop(0, steps)
    def _(s):
        for direction in range(4):

            @pl.when(senders[direction])
            def _():
                halo(s, direction).wait_send()

    for which in range(4):

        @pl.when((has_xu, has_xu, has_yu, has_yu)[which])
        def _():
            first(which).wait_send()


def per_device(pressure, vel_x, vel_y, vel_z, material, density_table, speed_table, panel_vals, panel_tile, panel_cell):
    size_x = lax.axis_size("gx")
    size_y = lax.axis_size("gy")
    devices = size_x * size_y
    cx, cy, nz = pressure.shape
    steps = panel_vals.shape[2]
    columns = panel_vals.shape[0] * panel_vals.shape[1]
    slots = max(2, 2 * columns // devices)
    per_chunk = max(1, 8 // slots)
    rows = slots * per_chunk
    chunks = steps // per_chunk
    group = LANES // rows
    plan = (size_x, size_y, slots, per_chunk, rows, group)
    f32 = jnp.float32
    vmem = pl.BlockSpec(memory_space=pltpu.VMEM)
    smem = pl.BlockSpec(memory_space=pltpu.SMEM)
    hbm = pl.BlockSpec(memory_space=pltpu.HBM)
    send, head = pl.pallas_call(
        functools.partial(pack_kernel, plan),
        out_shape=(
            jax.ShapeDtypeStruct((chunks, devices, rows, nz), f32),
            jax.ShapeDtypeStruct((devices, 1, LANES), f32),
        ),
        in_specs=[smem, smem, vmem],
        out_specs=(vmem, vmem),
        scratch_shapes=[pltpu.SMEM((devices,), jnp.int32)],
        compiler_params=pltpu.CompilerParams(vmem_limit_bytes=16 * 1024 * 1024),
        name="pack",
    )(panel_tile.reshape(-1), panel_cell, panel_vals.reshape(columns, steps, nz))
    field = jax.ShapeDtypeStruct((cx, cy, nz), f32)
    dma = pltpu.SemaphoreType.DMA
    return pl.pallas_call(
        functools.partial(wave_kernel, plan),
        out_shape=(field,) * 4,
        in_specs=[hbm] * 5 + [smem] * 2 + [vmem] * 2,
        out_specs=(vmem,) * 4,
        scratch_shapes=[
            pltpu.VMEM((cx, cy, nz), jnp.int32),
            pltpu.VMEM((cx, cy, nz), f32),
            pltpu.VMEM((cx, cy, nz), f32),
            pltpu.VMEM((chunks, devices, rows, nz), f32),
            pltpu.VMEM((devices, 1, LANES), f32),
            pltpu.VMEM((cx * cy, devices * rows), jnp.bfloat16),
            pltpu.VMEM((devices * rows, 2 * nz), jnp.bfloat16),
            pltpu.VMEM((cx * cy, nz), f32),
            pltpu.VMEM((steps, cy, nz), f32),
            pltpu.VMEM((steps, cy, nz), f32),
            pltpu.VMEM((steps, cx, 1, nz), f32),
            pltpu.VMEM((steps, cx, 1, nz), f32),
            pltpu.VMEM((steps, 2, cy, nz), f32),
            pltpu.VMEM((steps + 1, 2, cx, 1, nz), f32),
            pltpu.VMEM((cy, nz), f32),
            pltpu.VMEM((cy, nz), f32),
            pltpu.VMEM((cx, 1, nz), f32),
            pltpu.VMEM((cx, 1, nz), f32),
            pltpu.VMEM((cy, nz), f32),
            pltpu.VMEM((2, cx, 1, nz), f32),
            dma((5,)),
            dma((chunks,)),
            dma((chunks,)),
            dma((2,)),
            dma((steps, 4)),
            dma((steps, 4)),
            dma((4,)),
            dma((4,)),
        ],
        compiler_params=pltpu.CompilerParams(
            collective_id=0, has_side_effects=True, vmem_limit_bytes=40 * 1024 * 1024
        ),
        name="wave",
    )(pressure, vel_x, vel_y, vel_z, material, density_table, speed_table, send, head)


def solution(mesh):
    tile = P("gx", "gy", None)
    return jax.shard_map(
        per_device,
        mesh=mesh,
        in_specs=(
            tile,
            tile,
            tile,
            tile,
            tile,
            P(),
            P(),
            P(("gx", "gy"), None, None, None),
            P(("gx", "gy"), None, None),
            P(("gx", "gy"), None),
        ),
        out_specs=(tile,) * 4,
        check_vma=False,
    )
```
